512 devices in a mesh: dp: 4 (over z_hi), edata: 8 (over y), expert: 16 (over z_lo, x, core).
Axes of the slice: x: 4, y: 8, z: 8 (z_hi: 4, z_lo: 2; z = z_hi * 2 + z_lo), core: 2. Of those that a mesh axis runs over, the one named last changes fastest.
Arguments:
- out_grad: bfloat16 [65536, 7168], P(('dp', 'edata', 'expert')), may hold values from -6 to 6
- route_prob: float32 [65536, 2], P(('dp', 'edata', 'expert')), may hold values from 0.1 to 1
- expert_ids: int32 [65536, 2], P(('dp', 'edata', 'expert')), may hold values from 0 to 127, as said below
- slots: int32 [65536, 2], P(('dp', 'edata', 'expert')), may hold values from -1 to 3, as said below
- counts: int32 [512, 16], P(('dp', 'edata', 'expert')), may hold values from 0 to 4, as said below
- down_weight: bfloat16 [16, 2432, 7168], P('expert', 'dp', 'edata'), may hold values from -0.125 to 0.125
- saved_hidden: bfloat16 [16, 2048, 2432], P('expert', 'edata', 'dp'), may hold values from -0.29882812 to 0.29882812
Outputs:
- hidden_grad: bfloat16 [16, 2048, 2432], P('expert', 'edata', 'dp')
- weight_grad: bfloat16 [16, 2432, 7168], P('expert', 'dp', 'edata')
The draws below stay inside these ranges and needn't reach their ends.
Inputs may be any that keep to these rules, and one draw needn't show every extreme that they name: `expert_ids`: each token names two different experts. Expert k * 8 is window expert k; a token names at most one window expert. `slots`: for a token's window expert, the number of earlier tokens of its block of 128 that name the same expert; -1 for the other expert. Row g counts the tokens of block g of 128 that name each window expert; some window expert has 4 in every row.
All inputs are finite; a program needn't handle non-finite values.
Results may differ from the reference program's by a relative error of at most 0.017.
Values may be sent and summed in bfloat16 or wider, within the bound.
No kernel may reach another device: no remote copies, remote signals or barrier semaphores. Data moves between devices by JAX's collectives and lax.ppermute only.
A program may use at most 64 MiB of HBM per device.

```python
import jax
import jax.numpy as jnp
from jax import lax

D = 7168
FF_W = 2432
EXP_DEV = 8
CAP = 4
TOK_DEV = 128
FLIGHT = 16
TOKENS = 65536
ROWS = 2048
DBLOCK = 896


def routing(key):
    blocks = TOKENS // TOK_DEV
    subkeys = jax.random.split(key, 9)
    column = jnp.arange(FLIGHT, dtype=jnp.int32)
    tallies = jax.random.randint(subkeys[0], (blocks, FLIGHT), 0, CAP + 1)
    always_full = jax.random.randint(subkeys[1], (), 0, FLIGHT)
    single = jax.random.randint(subkeys[2], (blocks,), 0, FLIGHT)
    tallies = jnp.where((column[None, :] == always_full) | (column[None, :] == single[:, None]), CAP, tallies)
    block_ends = jnp.cumsum(tallies, axis=1)
    ordinal = jnp.arange(TOK_DEV, dtype=jnp.int32)
    owner_index = jnp.sum((block_ends[:, None, :] <= ordinal[None, :, None]).astype(jnp.int32), axis=2)
    shuffle = jax.vmap(lambda sub_key: jax.random.permutation(sub_key, TOK_DEV))(jax.random.split(subkeys[3], blocks))
    inverse = jnp.argsort(shuffle, axis=1)
    window = jnp.take_along_axis(owner_index, inverse, axis=1)
    onehot = (window[:, :, None] == column[None, None, :]).astype(jnp.int32)
    position = jnp.sum((jnp.cumsum(onehot, axis=1) - onehot) * onehot, axis=2)
    local_one = jax.random.randint(subkeys[4], (blocks, TOK_DEV), 1, EXP_DEV)
    owner_one = jax.random.randint(subkeys[5], (blocks, TOK_DEV), 0, FLIGHT)
    offset_step = jax.random.randint(subkeys[6], (blocks, TOK_DEV), 1, EXP_DEV - 1)
    local_two = 1 + (local_one - 1 + offset_step) % (EXP_DEV - 1)
    owner_two = jax.random.randint(subkeys[7], (blocks, TOK_DEV), 0, FLIGHT)
    chosen = window < FLIGHT
    first_id = jnp.where(chosen, window * EXP_DEV, owner_one * EXP_DEV + local_one)
    second_id = owner_two * EXP_DEV + local_two
    first_slot = jnp.where(chosen, position, -1)
    second_slot = jnp.full((blocks, TOK_DEV), -1, jnp.int32)
    flipped = jax.random.randint(subkeys[8], (blocks, TOK_DEV), 0, 2) == 1
    expert_table = jnp.stack([jnp.where(flipped, second_id, first_id), jnp.where(flipped, first_id, second_id)], axis=-1)
    slot_table = jnp.stack([jnp.where(flipped, second_slot, first_slot), jnp.where(flipped, first_slot, second_slot)], axis=-1)
    return (expert_table.reshape(TOKENS, 2).astype(jnp.int32), slot_table.reshape(TOKENS, 2).astype(jnp.int32), tallies.astype(jnp.int32))


def draw_expert_ids(key, part):
    expert_table, slot_table, tallies = routing(key)
    return expert_table


def draw_slots(key, part):
    expert_table, slot_table, tallies = routing(key)
    return slot_table


def draw_counts(key, part):
    expert_table, slot_table, tallies = routing(key)
    return tallies


def level_of(stream_key, shape, cuts, smallest, largest):
    def one(dim, blocks):
        steps = jax.random.uniform(jax.random.fold_in(jax.random.fold_in(stream_key, 6), dim), (blocks,), jnp.float32, smallest / len(cuts), largest / len(cuts))
        return jnp.repeat(jnp.exp(steps), shape[dim] // blocks).reshape((-1,) + (1,) * (len(shape) - dim - 1))

    loudness = one(*cuts[0])
    for cut in cuts[1:]:
        loudness = loudness * one(*cut)
    return loudness


def noise(own_key, shape, width, bound, shards=(), kind=jnp.bfloat16):
    result = width * jax.random.normal(own_key, shape, jnp.float32)
    if shards:
        result = result * level_of(own_key, shape, shards, -0.22, 0.18)
    return jnp.clip(result, -bound, bound).astype(kind)


def setup_inputs(seed: int = 0) -> dict:
    keys = jax.random.split(jax.random.key(seed), 8)
    out_grad = noise(keys[0], (TOKENS, D), 1.0, 6.0, ((0, 512),))
    route_prob = jnp.clip(0.1 + 0.9 * jax.random.uniform(keys[1], (TOKENS, 2), jnp.float32) ** level_of(keys[1], (TOKENS, 2), ((0, 512),), -0.2, 0.2), 0.1, 1.0)
    expert_ids = draw_expert_ids(jax.random.fold_in(keys[7], 71), 0)
    slots = draw_slots(jax.random.fold_in(keys[7], 71), 0)
    counts = draw_counts(jax.random.fold_in(keys[7], 71), 0)
    down_weight = noise(keys[5], (FLIGHT, FF_W, D), FF_W ** -0.5, 0.125, ((0, 16), (1, 4), (2, 8)))
    saved_hidden = noise(keys[6], (FLIGHT, ROWS, FF_W), 0.05, 0.29882812, ((0, 16), (1, 8), (2, 4)))
    return {"out_grad": out_grad, "route_prob": route_prob, "expert_ids": expert_ids, "slots": slots, "counts": counts, "down_weight": down_weight, "saved_hidden": saved_hidden}


def expert_terms(operands):
    slot_rows, weight, hidden = operands
    running = jnp.zeros((ROWS, FF_W), jnp.float32)
    for block_index in range(D // DBLOCK):
        first_col = block_index * DBLOCK
        partial_value = jnp.dot(slot_rows[:, first_col:first_col + DBLOCK], weight[:, first_col:first_col + DBLOCK].T, preferred_element_type=jnp.float32)
        rounded = lax.optimization_barrier(partial_value.astype(jnp.bfloat16))
        running = running + rounded.astype(jnp.float32)
    gradient = jnp.dot(hidden.T, slot_rows, preferred_element_type=jnp.float32)
    return running.astype(jnp.bfloat16), gradient.astype(jnp.bfloat16)


def reference(out_grad, route_prob, expert_ids, slots, counts, down_weight, saved_hidden):
    token_block = jnp.arange(TOKENS, dtype=jnp.int32) // TOK_DEV
    owner_index = expert_ids // EXP_DEV
    inside = expert_ids % EXP_DEV == 0
    safe_owner = jnp.minimum(owner_index, FLIGHT - 1).astype(jnp.int32)
    slot_limit = counts[token_block[:, None], safe_owner]
    usable = inside & (slots >= 0) & (slots < slot_limit)
    flat_slot = jnp.where(usable, safe_owner * ROWS + token_block[:, None] * CAP + slots, FLIGHT * ROWS).astype(jnp.int32)
    dispatched = jnp.zeros((FLIGHT * ROWS, D), jnp.bfloat16)
    for choice_index in range(2):
        scaled_rows = (route_prob[:, choice_index:choice_index + 1] * out_grad.astype(jnp.float32)).astype(jnp.bfloat16)
        dispatched = dispatched.at[flat_slot[:, choice_index]].add(scaled_rows, mode="drop")
    dispatched = dispatched.reshape(FLIGHT, ROWS, D)
    hidden_grad, weight_grad = lax.map(expert_terms, (dispatched, down_weight, saved_hidden))
    return hidden_grad, weight_grad
```

```python
import jax
import jax.numpy as jnp
from jax import lax
from jax.experimental import pallas as pl
from jax.experimental.pallas import tpu as pltpu
from jax.sharding import PartitionSpec as P

EXP_DEV = 8
CAP = 4
VMEM_LIMIT = 48 * 1024 * 1024


def dispatch_kernel(prob_ref, ids_ref, slots_ref, counts_ref, grad_ref, out_ref):
    rows = out_ref.shape[1]
    flight = counts_ref.shape[1]
    tokens = grad_ref.shape[0]
    own = lax.broadcasted_iota(jnp.int32, (rows, flight), 0) // CAP
    column = lax.broadcasted_iota(jnp.int32, (rows, flight), 1)
    limit = jnp.sum(jnp.where(own == column, counts_ref[...], 0), axis=1, keepdims=True)
    row = lax.broadcasted_iota(jnp.int32, (rows, tokens), 0)
    expert = (row // CAP) * EXP_DEV
    slot = row % CAP
    picker = jnp.zeros((rows, tokens), jnp.float32)
    scale = jnp.zeros((rows, 1), jnp.float32)
    for choice in range(2):
        match = (
            (ids_ref[choice : choice + 1, :] == expert)
            & (slots_ref[choice : choice + 1, :] == slot)
            & (slot < limit)
        )
        picker = picker + jnp.where(match, 1.0, 0.0)
        scale = scale + jnp.sum(
            jnp.where(match, prob_ref[choice : choice + 1, :], 0.0), axis=1, keepdims=True
        )
    picked = jnp.dot(
        picker.astype(jnp.bfloat16), grad_ref[...], preferred_element_type=jnp.float32
    )
    out_ref[0] = (picked * scale).astype(out_ref.dtype)


def dispatch(route_prob, expert_ids, slots, counts, out_grad, blocks):
    tokens, width = out_grad.shape
    flight = counts.shape[1]
    small = lambda shape: pl.BlockSpec(shape, lambda b: (0, 0))
    return pl.pallas_call(
        dispatch_kernel,
        grid=(blocks,),
        in_specs=[
            small((2, tokens)),
            small((2, tokens)),
            small((2, tokens)),
            small((1, flight)),
            pl.BlockSpec((tokens, width // blocks), lambda b: (0, b)),
        ],
        out_specs=pl.BlockSpec((1, flight * CAP, width // blocks), lambda b: (b, 0, 0)),
        out_shape=jax.ShapeDtypeStruct((blocks, flight * CAP, width // blocks), jnp.bfloat16),
        compiler_params=pltpu.CompilerParams(vmem_limit_bytes=VMEM_LIMIT),
    )(route_prob.T, expert_ids.T, slots.T, counts, out_grad)


def hidden_kernel(weight_ref, rows_ref, out_ref):
    out_ref[0] = lax.dot_general(
        weight_ref[...],
        rows_ref[0],
        (((1,), (1,)), ((), ())),
        preferred_element_type=jnp.float32,
    ).astype(out_ref.dtype)


def hidden_partial(weight, rows):
    units, width = weight.shape
    parts, slots, _ = rows.shape
    return pl.pallas_call(
        hidden_kernel,
        grid=(parts,),
        in_specs=[
            pl.BlockSpec((units, width), lambda b: (0, 0)),
            pl.BlockSpec((1, slots, width), lambda b: (b, 0, 0)),
        ],
        out_specs=pl.BlockSpec((1, units, slots), lambda b: (b, 0, 0)),
        out_shape=jax.ShapeDtypeStruct((parts, units, slots), jnp.bfloat16),
        compiler_params=pltpu.CompilerParams(vmem_limit_bytes=VMEM_LIMIT),
    )(weight, rows)


def weight_kernel(hidden_ref, rows_ref, out_ref, total):
    step = pl.program_id(0)

    @pl.when(step == 0)
    def _():
        total[...] = jnp.zeros_like(total)

    total[...] += jnp.dot(hidden_ref[0], rows_ref[0], preferred_element_type=jnp.float32)

    @pl.when(step == pl.num_programs(0) - 1)
    def _():
        out_ref[...] = total[...].astype(out_ref.dtype)


def weight_grad(hidden, rows):
    parts, units, slots = hidden.shape
    width = rows.shape[2]
    return pl.pallas_call(
        weight_kernel,
        grid=(parts,),
        in_specs=[
            pl.BlockSpec((1, units, slots), lambda b: (b, 0, 0)),
            pl.BlockSpec((1, slots, width), lambda b: (b, 0, 0)),
        ],
        out_specs=pl.BlockSpec((units, width), lambda b: (0, 0)),
        out_shape=jax.ShapeDtypeStruct((units, width), jnp.bfloat16),
        scratch_shapes=[pltpu.VMEM((units, width), jnp.float32)],
        compiler_params=pltpu.CompilerParams(vmem_limit_bytes=VMEM_LIMIT),
    )(hidden, rows)


def per_device(out_grad, route_prob, expert_ids, slots, counts, down_weight, saved_hidden):
    flight = lax.axis_size("expert")
    edata = lax.axis_size("edata")
    dp = lax.axis_size("dp")
    own_slots = saved_hidden.shape[1]
    width = out_grad.shape[1] // edata
    outgoing = dispatch(route_prob, expert_ids, slots, counts, out_grad, edata)
    arrived = lax.all_to_all(
        outgoing.reshape(edata * flight, CAP, width),
        ("edata", "expert"),
        split_axis=0,
        concat_axis=0,
        tiled=True,
    )
    rows = lax.all_gather(arrived.reshape(edata * flight * CAP, width), "dp", axis=0)
    rows = rows.reshape(edata, own_slots, width)
    hidden = lax.all_gather(saved_hidden[0].T, "edata", axis=0)
    partial = hidden_partial(down_weight[0], rows)
    hidden_grad = lax.psum_scatter(partial, "edata", scatter_dimension=0, tiled=False)
    grad = weight_grad(hidden, rows)
    return hidden_grad.T[None], grad[None]


def solution(mesh):
    placed = (
        P(("dp", "edata", "expert"), None),
        P(("dp", "edata", "expert"), None),
        P(("dp", "edata", "expert"), None),
        P(("dp", "edata", "expert"), None),
        P(("dp", "edata", "expert"), None),
        P("expert", "dp", "edata"),
        P("expert", "edata", "dp"),
    )
    return jax.shard_map(
        per_device,
        mesh=mesh,
        in_specs=placed,
        out_specs=(P("expert", "edata", "dp"), P("expert", "dp", "edata")),
        check_vma=False,
    )
```

```python
import jax
import jax.numpy as jnp
from jax import lax
from jax.experimental import pallas as pl
from jax.experimental.pallas import tpu as pltpu
from jax.sharding import PartitionSpec as P

EXP_DEV = 8
CAP = 4
PARTS = 8
QUARTERS = 4
VMEM_LIMIT = 60 * 1024 * 1024


def full(count):
    return [pl.BlockSpec(memory_space=pltpu.VMEM)] * count


def lying(count):
    return [pl.BlockSpec(memory_space=pltpu.HBM)] * count


def params():
    return pltpu.CompilerParams(vmem_limit_bytes=VMEM_LIMIT)


def dispatch_kernel(prob_ref, ids_ref, slots_ref, counts_ref, grad_ref, out_ref, *scratch):
    prob_v, ids_v, slots_v, counts_v, grad_v, sems = scratch
    blocks, rows, width = out_ref.shape
    flight = counts_v.shape[1]
    tokens = grad_v.shape[1]
    copies = [
        pltpu.make_async_copy(source, place, sems.at[index])
        for index, (source, place) in enumerate(
            ((ids_ref, ids_v), (slots_ref, slots_v), (counts_ref, counts_v), (prob_ref, prob_v))
        )
    ]
    for block in range(blocks):
        copies.append(
            pltpu.make_async_copy(
                grad_ref.at[:, pl.ds(block * width, width)], grad_v.at[block], sems.at[4 + block]
            )
        )
    for copy in copies:
        copy.start()
    own = lax.broadcasted_iota(jnp.int32, (rows, flight), 0) // CAP
    column = lax.broadcasted_iota(jnp.int32, (rows, flight), 1)
    row = lax.broadcasted_iota(jnp.int32, (rows, tokens), 0)
    expert = (row // CAP) * EXP_DEV
    slot = row % CAP
    for copy in copies[:4]:
        copy.wait()
    limit = jnp.sum(jnp.where(own == column, counts_v[...], 0), axis=1, keepdims=True)
    picker = jnp.zeros((rows, tokens), jnp.float32)
    scale = jnp.zeros((rows, 1), jnp.float32)
    for choice in range(2):
        match = (
            (ids_v[choice : choice + 1, :] == expert)
            & (slots_v[choice : choice + 1, :] == slot)
            & (slot < limit)
        )
        picker = picker + jnp.where(match, 1.0, 0.0)
        scale = scale + jnp.sum(
            jnp.where(match, prob_v[choice : choice + 1, :], 0.0), axis=1, keepdims=True
        )
    picker = picker.astype(jnp.bfloat16)
    for block in range(blocks):
        copies[4 + block].wait()
        picked = jnp.dot(picker, grad_v[block], preferred_element_type=jnp.float32)
        out_ref[block] = (picked * scale).astype(out_ref.dtype)


def dispatch(route_prob, expert_ids, slots, counts, out_grad, blocks):
    tokens, model = out_grad.shape
    flight = counts.shape[1]
    width = model // blocks
    return pl.pallas_call(
        dispatch_kernel,
        in_specs=lying(5),
        out_specs=full(1)[0],
        out_shape=jax.ShapeDtypeStruct((blocks, flight * CAP, width), jnp.bfloat16),
        scratch_shapes=[
            pltpu.VMEM((2, tokens), jnp.float32),
            pltpu.VMEM((2, tokens), jnp.int32),
            pltpu.VMEM((2, tokens), jnp.int32),
            pltpu.VMEM((1, flight), jnp.int32),
            pltpu.VMEM((blocks, tokens, width), jnp.bfloat16),
            pltpu.SemaphoreType.DMA((4 + blocks,)),
        ],
        compiler_params=params(),
    )(route_prob.T, expert_ids.T, slots.T, counts, out_grad)


def turn_kernel(weight_ref, out_ref):
    out_ref[...] = weight_ref[...].T


def turn(weight):
    units, width = weight.shape
    return pl.pallas_call(
        turn_kernel,
        in_specs=full(1),
        out_specs=full(1)[0],
        out_shape=jax.ShapeDtypeStruct((width, units), weight.dtype),
        compiler_params=params(),
    )(weight)


def hidden_kernel(weight_ref, *refs):
    count = len(refs) - 6
    pieces = refs[:count]
    out_ref, weight_v, rows_v, result_v, sems, out_sems = refs[count:]
    _, parts, slots, units = result_v.shape
    load = pltpu.make_async_copy(weight_ref, weight_v, sems.at[count])
    load.start()
    copies = [
        pltpu.make_async_copy(piece, rows_v.at[index], sems.at[index])
        for index, piece in enumerate(pieces)
    ]
    for copy in copies:
        copy.start()
    load.wait()
    stores = []
    for index in range(count):
        copies[index].wait()
        product = jnp.dot(rows_v[index], weight_v[...], preferred_element_type=jnp.float32)
        result_v[index] = product.astype(result_v.dtype).reshape(parts, slots, units)
        stores.append(
            pltpu.make_async_copy(
                result_v.at[index], out_ref.at[:, pl.ds(index * slots, slots)], out_sems.at[index]
            )
        )
        stores[-1].start()
    for store in stores:
        store.wait()


def hidden_partial(weight, pieces):
    width, units = weight.shape
    rows = pieces[0].shape[0]
    count = len(pieces)
    slots = rows // PARTS
    return pl.pallas_call(
        hidden_kernel,
        in_specs=lying(1 + count),
        out_specs=lying(1)[0],
        out_shape=jax.ShapeDtypeStruct((PARTS, count * slots, units), jnp.bfloat16),
        scratch_shapes=[
            pltpu.VMEM((width, units), jnp.bfloat16),
            pltpu.VMEM((count, rows, width), jnp.bfloat16),
            pltpu.VMEM((count, PARTS, slots, units), jnp.bfloat16),
            pltpu.SemaphoreType.DMA((count + 1,)),
            pltpu.SemaphoreType.DMA((count,)),
        ],
        compiler_params=params(),
    )(weight, *pieces)


def weight_kernel(hidden_ref, *refs):
    pieces = refs[:-4]
    out_ref, rows_v, hidden_v, sems = refs[-4:]
    parts, _, size = hidden_ref.shape
    slots = size // len(pieces)
    copies = []
    for part in range(parts):
        copies.append(
            pltpu.make_async_copy(
                hidden_ref.at[part], hidden_v.at[:, pl.ds(part * size, size)], sems.at[0, part]
            )
        )
        for index, piece in enumerate(pieces):
            copies.append(
                pltpu.make_async_copy(
                    piece.at[pl.ds(part * slots, slots)],
                    rows_v.at[pl.ds(part * size + index * slots, slots)],
                    sems.at[1 + index, part],
                )
            )
    for copy in copies:
        copy.start()
    for copy in copies:
        copy.wait()
    out_ref[...] = jnp.dot(
        hidden_v[...], rows_v[...], preferred_element_type=jnp.float32
    ).astype(out_ref.dtype)


def weight_grad(hidden, pieces):
    parts, units, size = hidden.shape
    width = pieces[0].shape[1]
    return pl.pallas_call(
        weight_kernel,
        in_specs=lying(1 + len(pieces)),
        out_specs=full(1)[0],
        out_shape=jax.ShapeDtypeStruct((units, width), jnp.bfloat16),
        scratch_shapes=[
            pltpu.VMEM((parts * size, width), jnp.bfloat16),
            pltpu.VMEM((units, parts * size), jnp.bfloat16),
            pltpu.SemaphoreType.DMA((1 + len(pieces), parts)),
        ],
        compiler_params=params(),
    )(hidden, *pieces)


def finish_kernel(sums_ref, last_ref, out_ref):
    last = jnp.sum(last_ref[...].astype(jnp.float32), axis=0).astype(jnp.bfloat16)
    joined = jnp.concatenate([sums_ref[...], last], axis=0)
    size = joined.shape[0]
    first = lax.broadcasted_iota(jnp.int32, (size, size), 0)
    second = lax.broadcasted_iota(jnp.int32, (size, size), 1)
    same = jnp.where(first == second, 1.0, 0.0).astype(jnp.bfloat16)
    out_ref[...] = lax.dot_general(
        joined, same, (((0,), (0,)), ((), ())), preferred_element_type=jnp.float32
    ).astype(out_ref.dtype)


def finish(sums, last):
    slots, units = sums.shape
    return pl.pallas_call(
        finish_kernel,
        in_specs=full(2),
        out_specs=full(1)[0],
        out_shape=jax.ShapeDtypeStruct((units, slots + last.shape[1]), jnp.bfloat16),
        compiler_params=params(),
    )(sums, last)


def per_device(out_grad, route_prob, expert_ids, slots, counts, down_weight, saved_hidden):
    flight = lax.axis_size("expert")
    edata = lax.axis_size("edata")
    width = out_grad.shape[1] // edata
    outgoing = dispatch(route_prob, expert_ids, slots, counts, out_grad, edata)
    arrived = lax.all_to_all(
        outgoing.reshape(edata * flight, CAP, width),
        ("edata", "expert"),
        split_axis=0,
        concat_axis=0,
        tiled=True,
    )
    arrived, hidden, weight = lax.optimization_barrier(
        (arrived, saved_hidden[0].T, turn(down_weight[0]))
    )
    hidden = lax.all_gather(hidden, "edata", axis=0)
    blocks = arrived.reshape(2, QUARTERS, -1, width)
    quarters = [blocks[:, index].reshape(-1, width) for index in range(QUARTERS)]
    gathered = [lax.all_gather(quarter, "dp", axis=0, tiled=True) for quarter in quarters[:2]]
    third, hidden = lax.optimization_barrier((quarters[2], hidden))
    gathered.append(lax.all_gather(third, "dp", axis=0, tiled=True))
    partial = hidden_partial(weight, gathered)
    partial, fourth = lax.optimization_barrier((partial, quarters[3]))
    sums = lax.psum_scatter(partial, "edata", scatter_dimension=0, tiled=False)
    gathered.append(lax.all_gather(fourth, "dp", axis=0, tiled=True))
    spread = lax.all_to_all(
        hidden_partial(weight, gathered[3:]), "edata", split_axis=0, concat_axis=0, tiled=True
    )
    grad = weight_grad(hidden, gathered)
    return finish(sums, spread).T[None], grad[None]


def solution(mesh):
    placed = (
        P(("dp", "edata", "expert"), None),
        P(("dp", "edata", "expert"), None),
        P(("dp", "edata", "expert"), None),
        P(("dp", "edata", "expert"), None),
        P(("dp", "edata", "expert"), None),
        P("expert", "dp", "edata"),
        P("expert", "edata", "dp"),
    )
    return jax.shard_map(
        per_device,
        mesh=mesh,
        in_specs=placed,
        out_specs=(P("expert", "edata", "dp"), P("expert", "dp", "edata")),
        check_vma=False,
    )
```

```python
import jax
import jax.numpy as jnp
from jax import lax
from jax.experimental import pallas as pl
from jax.experimental.pallas import tpu as pltpu
from jax.sharding import PartitionSpec as P

EXP_DEV = 8
CAP = 4
PARTS = 8
QUARTERS = 4
VMEM_LIMIT = 60 * 1024 * 1024


def full(count):
    return [pl.BlockSpec(memory_space=pltpu.VMEM)] * count


def lying(count):
    return [pl.BlockSpec(memory_space=pl.ANY)] * count


def scalar():
    return [pl.BlockSpec(memory_space=pltpu.SMEM)]


def params():
    return pltpu.CompilerParams(vmem_limit_bytes=VMEM_LIMIT)


def dispatch_kernel(prob_ref, ids_ref, slots_ref, counts_ref, grad_ref, out_ref, *scratch):
    prob_v, ids_v, slots_v, counts_v, grad_v, sems = scratch
    width = out_ref.shape[2]
    flight = counts_v.shape[1]
    rows = flight * CAP
    blocks = out_ref.shape[0] // flight
    tokens = grad_v.shape[1]
    copies = [
        pltpu.make_async_copy(source, place, sems.at[index])
        for index, (source, place) in enumerate(
            ((ids_ref, ids_v), (slots_ref, slots_v), (counts_ref, counts_v), (prob_ref, prob_v))
        )
    ]
    for block in range(blocks):
        copies.append(
            pltpu.make_async_copy(
                grad_ref.at[:, pl.ds(block * width, width)], grad_v.at[block], sems.at[4 + block]
            )
        )
    for copy in copies:
        copy.start()
    own = lax.broadcasted_iota(jnp.int32, (rows, flight), 0) // CAP
    column = lax.broadcasted_iota(jnp.int32, (rows, flight), 1)
    row = lax.broadcasted_iota(jnp.int32, (rows, tokens), 0)
    expert = (row // CAP) * EXP_DEV
    slot = row % CAP
    for copy in copies[:4]:
        copy.wait()
    limit = jnp.sum(jnp.where(own == column, counts_v[...], 0), axis=1, keepdims=True)
    picker = jnp.zeros((rows, tokens), jnp.float32)
    scale = jnp.zeros((rows, 1), jnp.float32)
    for choice in range(2):
        match = (
            (ids_v[choice : choice + 1, :] == expert)
            & (slots_v[choice : choice + 1, :] == slot)
            & (slot < limit)
        )
        picker = picker + jnp.where(match, 1.0, 0.0)
        scale = scale + jnp.sum(
            jnp.where(match, prob_v[choice : choice + 1, :], 0.0), axis=1, keepdims=True
        )
    picker = picker.astype(jnp.bfloat16)
    for block in range(blocks):
        copies[4 + block].wait()
        picked = jnp.dot(picker, grad_v[block], preferred_element_type=jnp.float32)
        out_ref[block * flight : (block + 1) * flight] = (
            (picked * scale).reshape(flight, CAP, width).astype(out_ref.dtype)
        )


def dispatch(route_prob, expert_ids, slots, counts, out_grad, blocks):
    tokens, model = out_grad.shape
    flight = counts.shape[1]
    width = model // blocks
    return pl.pallas_call(
        dispatch_kernel,
        in_specs=lying(5),
        out_specs=full(1)[0],
        out_shape=jax.ShapeDtypeStruct((blocks * flight, CAP, width), jnp.bfloat16),
        scratch_shapes=[
            pltpu.VMEM((2, tokens), jnp.float32),
            pltpu.VMEM((2, tokens), jnp.int32),
            pltpu.VMEM((2, tokens), jnp.int32),
            pltpu.VMEM((1, flight), jnp.int32),
            pltpu.VMEM((blocks, tokens, width), jnp.bfloat16),
            pltpu.SemaphoreType.DMA((4 + blocks,)),
        ],
        compiler_params=params(),
    )(route_prob.T, expert_ids.T, slots.T, counts, out_grad)


def turn_kernel(weight_ref, out_ref):
    out_ref[...] = weight_ref[...].T


def turn(weight):
    units, width = weight.shape
    return pl.pallas_call(
        turn_kernel,
        in_specs=full(1),
        out_specs=full(1)[0],
        out_shape=jax.ShapeDtypeStruct((width, units), weight.dtype),
        compiler_params=params(),
    )(weight)


def place_of(place, shift):
    return lax.rem(place + shift, PARTS // 2) * 2


def near_kernel(place_ref, weight_ref, *refs):
    pieces = refs[:6]
    out_ref, weight_v, near_v, near_out, sems, out_sems = refs[6:]
    _, half, units = out_ref.shape
    load = pltpu.make_async_copy(weight_ref, weight_v, sems.at[6])
    load.start()
    copies = [
        pltpu.make_async_copy(
            piece, near_v.at[index // 2, pl.ds(index % 2 * half, half)], sems.at[index]
        )
        for index, piece in enumerate(pieces)
    ]
    for copy in copies:
        copy.start()
    load.wait()
    stores = []
    for index, shift in enumerate((0, 3, 1)):
        copies[2 * index].wait()
        copies[2 * index + 1].wait()
        near_out[index] = (
            jnp.dot(near_v[index], weight_v[...], preferred_element_type=jnp.float32)
            .astype(near_out.dtype)
            .reshape(2, half, units)
        )
        stores.append(
            pltpu.make_async_copy(
                near_out.at[index],
                out_ref.at[pl.ds(place_of(place_ref[0], shift), 2)],
                out_sems.at[index],
            )
        )
        stores[-1].start()
    for store in stores:
        store.wait()


def near_partial(place, weight, near):
    width, units = weight.shape
    half = near[0].shape[0]
    return pl.pallas_call(
        near_kernel,
        in_specs=scalar() + lying(7),
        out_specs=lying(1)[0],
        out_shape=jax.ShapeDtypeStruct((PARTS, half, units), jnp.bfloat16),
        scratch_shapes=[
            pltpu.VMEM((width, units), jnp.bfloat16),
            pltpu.VMEM((3, 2 * half, width), jnp.bfloat16),
            pltpu.VMEM((3, 2, half, units), jnp.bfloat16),
            pltpu.SemaphoreType.DMA((7,)),
            pltpu.SemaphoreType.DMA((3,)),
        ],
        compiler_params=params(),
    )(place, weight, *near)


def far_kernel(place_ref, weight_ref, first_ref, second_ref, _, out_ref, *scratch):
    weight_v, far_v, far_out, sems = scratch
    half, units = far_out.shape[1:]
    copies = [
        pltpu.make_async_copy(weight_ref, weight_v, sems.at[0]),
        pltpu.make_async_copy(first_ref, far_v.at[pl.ds(0, half)], sems.at[1]),
        pltpu.make_async_copy(second_ref, far_v.at[pl.ds(half, half)], sems.at[2]),
    ]
    for copy in copies:
        copy.start()
    for copy in copies:
        copy.wait()
    far_out[...] = (
        jnp.dot(far_v[...], weight_v[...], preferred_element_type=jnp.float32)
        .astype(far_out.dtype)
        .reshape(2, half, units)
    )
    store = pltpu.make_async_copy(
        far_out, out_ref.at[pl.ds(place_of(place_ref[0], 2), 2)], sems.at[3]
    )
    store.start()
    store.wait()


def far_partial(place, weight, far, partial):
    width, units = weight.shape
    half = far[0].shape[0]
    return pl.pallas_call(
        far_kernel,
        in_specs=scalar() + lying(4),
        out_specs=lying(1)[0],
        out_shape=jax.ShapeDtypeStruct(partial.shape, partial.dtype),
        scratch_shapes=[
            pltpu.VMEM((width, units), jnp.bfloat16),
            pltpu.VMEM((2 * half, width), jnp.bfloat16),
            pltpu.VMEM((2, half, units), jnp.bfloat16),
            pltpu.SemaphoreType.DMA((4,)),
        ],
        input_output_aliases={4: 0},
        compiler_params=params(),
    )(place, weight, *far, partial)


def last_kernel(weight_ref, rows_ref, out_ref):
    out_ref[...] = (
        jnp.dot(rows_ref[...], weight_ref[...], preferred_element_type=jnp.float32)
        .astype(out_ref.dtype)
        .reshape(out_ref.shape)
    )


def last_partial(weight, rows):
    return pl.pallas_call(
        last_kernel,
        in_specs=full(2),
        out_specs=full(1)[0],
        out_shape=jax.ShapeDtypeStruct(
            (PARTS, rows.shape[0] // PARTS, weight.shape[1]), jnp.bfloat16
        ),
        compiler_params=params(),
    )(weight, rows)


def weight_kernel(place_ref, hidden_ref, *refs):
    near, pieces = refs[:8], refs[8:-4]
    out_ref, rows_v, hidden_v, sems = refs[-4:]
    parts, _, size = hidden_ref.shape
    half = near[0].shape[0]
    slots = (size - half) // len(pieces)
    copies = []

    def fetch(piece, target, start, count, number):
        row = pl.multiple_of(target * size + start, slots)
        copies.append(
            pltpu.make_async_copy(
                piece, rows_v.at[pl.ds(row, count)], sems.at[number // parts, number % parts]
            )
        )

    for part in range(parts):
        copies.append(
            pltpu.make_async_copy(
                hidden_ref.at[part], hidden_v.at[:, pl.ds(part * size, size)], sems.at[0, part]
            )
        )
        for index, piece in enumerate(pieces):
            fetch(
                piece.at[pl.ds(part * slots, slots)],
                part,
                half + index * slots,
                slots,
                parts * (1 + index) + part,
            )
    for index, piece in enumerate(near):
        target = place_of(place_ref[0], (0, 3, 1, 2)[index // 2]) + index % 2
        fetch(piece, target, 0, half, parts * (1 + len(pieces)) + index)
    for copy in copies:
        copy.start()
    for copy in copies:
        copy.wait()
    out_ref[...] = jnp.dot(
        hidden_v[...], rows_v[...], preferred_element_type=jnp.float32
    ).astype(out_ref.dtype)


def weight_grad(place, hidden, near, far, pieces):
    parts, units, size = hidden.shape
    width = pieces[0].shape[1]
    return pl.pallas_call(
        weight_kernel,
        in_specs=scalar() + lying(9 + len(pieces)),
        out_specs=full(1)[0],
        out_shape=jax.ShapeDtypeStruct((units, width), jnp.bfloat16),
        scratch_shapes=[
            pltpu.VMEM((parts * size, width), jnp.bfloat16),
            pltpu.VMEM((units, parts * size), jnp.bfloat16),
            pltpu.SemaphoreType.DMA((2 + len(pieces), parts)),
        ],
        compiler_params=params(),
    )(place, hidden, *near, *far, *pieces)


def finish_kernel(sums_ref, last_ref, out_ref):
    last = jnp.sum(last_ref[...].astype(jnp.float32), axis=0).astype(jnp.bfloat16)
    joined = jnp.concatenate([sums_ref[...], last], axis=0)
    size = joined.shape[0]
    first = lax.broadcasted_iota(jnp.int32, (size, size), 0)
    second = lax.broadcasted_iota(jnp.int32, (size, size), 1)
    same = jnp.where(first == second, 1.0, 0.0).astype(jnp.bfloat16)
    out_ref[...] = lax.dot_general(
        joined, same, (((0,), (0,)), ((), ())), preferred_element_type=jnp.float32
    ).astype(out_ref.dtype)


def finish(sums, last):
    slots, units = sums.shape
    return pl.pallas_call(
        finish_kernel,
        in_specs=full(2),
        out_specs=full(1)[0],
        out_shape=jax.ShapeDtypeStruct((units, slots + last.shape[1]), jnp.bfloat16),
        compiler_params=params(),
    )(sums, last)


def shifted(value, axis, step):
    size = lax.axis_size(axis)
    return lax.ppermute(value, axis, [(i, (i + step) % size) for i in range(size)])


def per_device(out_grad, route_prob, expert_ids, slots, counts, down_weight, saved_hidden):
    flight = lax.axis_size("expert")
    edata = lax.axis_size("edata")
    width = out_grad.shape[1] // edata
    place = lax.axis_index("dp").astype(jnp.int32)[None]
    outgoing = dispatch(route_prob, expert_ids, slots, counts, out_grad, edata)
    arrived = lax.all_to_all(
        outgoing,
        ("edata", "expert"),
        split_axis=0,
        concat_axis=0,
        tiled=True,
    )
    arrived, hidden, weight = lax.optimization_barrier(
        (arrived, saved_hidden[0].T, turn(down_weight[0]))
    )
    hidden = lax.all_gather(hidden, "edata", axis=0)
    blocks = arrived.reshape(2, QUARTERS, -1, width)
    first = blocks[0, :3].reshape(-1, width)
    second = blocks[1, :3].reshape(-1, width)
    fourth = blocks[:, 3].reshape(-1, width)
    low_first = shifted(first, "dp", 1)
    high_second = shifted(second, "dp", -1)
    low_second = shifted(second, "dp", 1)
    high_first = shifted(first, "dp", -1)
    far = (shifted(low_first, "dp", 1), shifted(high_second, "dp", -1))
    near = (first, second, low_first, low_second, high_first, high_second)
    partial = near_partial(place, weight, near)
    partial = far_partial(place, weight, far, partial)
    partial, fourth, hidden = lax.optimization_barrier((partial, fourth, hidden))
    sums = lax.psum_scatter(partial, "edata", scatter_dimension=0, tiled=False)
    fourth = lax.all_gather(fourth, "dp", axis=0, tiled=True)
    spread = lax.all_to_all(
        last_partial(weight, fourth), "edata", split_axis=0, concat_axis=0, tiled=True
    )
    grad = weight_grad(place, hidden, near, far, (fourth,))
    return finish(sums, spread).T[None], grad[None]


def solution(mesh):
    placed = (
        P(("dp", "edata", "expert"), None),
        P(("dp", "edata", "expert"), None),
        P(("dp", "edata", "expert"), None),
        P(("dp", "edata", "expert"), None),
        P(("dp", "edata", "expert"), None),
        P("expert", "dp", "edata"),
        P("expert", "edata", "dp"),
    )
    return jax.shard_map(
        per_device,
        mesh=mesh,
        in_specs=placed,
        out_specs=(P("expert", "edata", "dp"), P("expert", "dp", "edata")),
        check_vma=False,
    )
```

```python
import jax
import jax.numpy as jnp
from jax import lax
from jax.experimental import pallas as pl
from jax.experimental.pallas import tpu as pltpu
from jax.sharding import PartitionSpec as P

EXP_DEV = 8
CAP = 4
PARTS = 8
QUARTERS = 4
VMEM_LIMIT = 60 * 1024 * 1024
VMEM_LITTLE = 20 * 1024 * 1024


def full(count):
    return [pl.BlockSpec(memory_space=pltpu.VMEM)] * count


def lying(count):
    return [pl.BlockSpec(memory_space=pl.ANY)] * count


def scalar():
    return [pl.BlockSpec(memory_space=pltpu.SMEM)]


def params(limit=VMEM_LIMIT):
    return pltpu.CompilerParams(vmem_limit_bytes=limit)


def dispatch_kernel(prob_ref, ids_ref, slots_ref, counts_ref, grad_ref, out_ref, *scratch):
    prob_v, ids_v, slots_v, counts_v, grad_v, out_v, sems, out_sems = scratch
    width = out_ref.shape[2]
    flight = counts_v.shape[1]
    rows = flight * CAP
    blocks = out_ref.shape[0] // flight
    tokens = grad_v.shape[1]
    copies = [
        pltpu.make_async_copy(source, place, sems.at[index])
        for index, (source, place) in enumerate(
            ((ids_ref, ids_v), (slots_ref, slots_v), (counts_ref, counts_v), (prob_ref, prob_v))
        )
    ]
    for block in range(blocks):
        copies.append(
            pltpu.make_async_copy(
                grad_ref.at[:, pl.ds(block * width, width)], grad_v.at[block], sems.at[4 + block]
            )
        )
    for copy in copies:
        copy.start()
    own = lax.broadcasted_iota(jnp.int32, (rows, flight), 0) // CAP
    column = lax.broadcasted_iota(jnp.int32, (rows, flight), 1)
    row = lax.broadcasted_iota(jnp.int32, (rows, tokens), 0)
    expert = (row // CAP) * EXP_DEV
    slot = row % CAP
    for copy in copies[:4]:
        copy.wait()
    limit = jnp.sum(jnp.where(own == column, counts_v[...], 0), axis=1, keepdims=True)
    picker = jnp.zeros((rows, tokens), jnp.float32)
    scale = jnp.zeros((rows, 1), jnp.float32)
    for choice in range(2):
        match = (
            (ids_v[choice : choice + 1, :] == expert)
            & (slots_v[choice : choice + 1, :] == slot)
            & (slot < limit)
        )
        picker = picker + jnp.where(match, 1.0, 0.0)
        scale = scale + jnp.sum(
            jnp.where(match, prob_v[choice : choice + 1, :], 0.0), axis=1, keepdims=True
        )
    picker = picker.astype(jnp.bfloat16)
    stores = []
    for block in range(blocks):
        copies[4 + block].wait()
        picked = jnp.dot(picker, grad_v[block], preferred_element_type=jnp.float32)
        window = pl.ds(block * flight, flight)
        out_v[window] = (picked * scale).reshape(flight, CAP, width).astype(out_v.dtype)
        stores.append(
            pltpu.make_async_copy(out_v.at[window], out_ref.at[window], out_sems.at[block])
        )
        stores[-1].start()
    for store in stores:
        store.wait()


def dispatch(route_prob, expert_ids, slots, counts, out_grad, blocks):
    tokens, model = out_grad.shape
    flight = counts.shape[1]
    width = model // blocks
    return pl.pallas_call(
        dispatch_kernel,
        in_specs=lying(5),
        out_specs=lying(1)[0],
        out_shape=jax.ShapeDtypeStruct((blocks * flight, CAP, width), jnp.bfloat16),
        scratch_shapes=[
            pltpu.VMEM((2, tokens), jnp.float32),
            pltpu.VMEM((2, tokens), jnp.int32),
            pltpu.VMEM((2, tokens), jnp.int32),
            pltpu.VMEM((1, flight), jnp.int32),
            pltpu.VMEM((blocks, tokens, width), jnp.bfloat16),
            pltpu.VMEM((blocks * flight, CAP, width), jnp.bfloat16),
            pltpu.SemaphoreType.DMA((4 + blocks,)),
            pltpu.SemaphoreType.DMA((blocks,)),
        ],
        compiler_params=params(),
    )(route_prob.T, expert_ids.T, slots.T, counts, out_grad)


def turn_kernel(weight_ref, out_ref):
    out_ref[...] = weight_ref[...].T


def turn(weight):
    units, width = weight.shape
    return pl.pallas_call(
        turn_kernel,
        in_specs=full(1),
        out_specs=full(1)[0],
        out_shape=jax.ShapeDtypeStruct((width, units), weight.dtype),
        compiler_params=params(),
    )(weight)


def place_of(place, shift):
    return lax.rem(place + shift, PARTS // 2) * 2


def near_kernel(place_ref, weight_ref, *refs):
    pieces = refs[:6]
    out_ref, weight_v, near_v, near_out, sems, out_sems = refs[6:]
    _, half, units = out_ref.shape
    load = pltpu.make_async_copy(weight_ref, weight_v, sems.at[6])
    load.start()
    copies = [
        pltpu.make_async_copy(
            piece, near_v.at[index // 2, pl.ds(index % 2 * half, half)], sems.at[index]
        )
        for index, piece in enumerate(pieces)
    ]
    for copy in copies:
        copy.start()
    load.wait()
    stores = []
    for index, shift in enumerate((0, 3, 1)):
        copies[2 * index].wait()
        copies[2 * index + 1].wait()
        near_out[index] = (
            jnp.dot(near_v[index], weight_v[...], preferred_element_type=jnp.float32)
            .astype(near_out.dtype)
            .reshape(2, half, units)
        )
        stores.append(
            pltpu.make_async_copy(
                near_out.at[index],
                out_ref.at[pl.ds(place_of(place_ref[0], shift), 2)],
                out_sems.at[index],
            )
        )
        stores[-1].start()
    for store in stores:
        store.wait()


def near_partial(place, weight, near):
    width, units = weight.shape
    half = near[0].shape[0]
    return pl.pallas_call(
        near_kernel,
        in_specs=scalar() + lying(7),
        out_specs=lying(1)[0],
        out_shape=jax.ShapeDtypeStruct((PARTS, half, units), jnp.bfloat16),
        scratch_shapes=[
            pltpu.VMEM((width, units), jnp.bfloat16),
            pltpu.VMEM((3, 2 * half, width), jnp.bfloat16),
            pltpu.VMEM((3, 2, half, units), jnp.bfloat16),
            pltpu.SemaphoreType.DMA((7,)),
            pltpu.SemaphoreType.DMA((3,)),
        ],
        compiler_params=params(),
    )(place, weight, *near)


def far_kernel(place_ref, weight_ref, first_ref, second_ref, _, out_ref, *scratch):
    weight_v, far_v, far_out, sems = scratch
    target = place_of(place_ref[0], 2)
    load = pltpu.make_async_copy(weight_ref, weight_v, sems.at[0])
    load.start()
    copies = [
        pltpu.make_async_copy(piece, far_v.at[half], sems.at[1 + half])
        for half, piece in enumerate((first_ref, second_ref))
    ]
    for copy in copies:
        copy.start()
    load.wait()
    stores = []
    for half in range(2):
        copies[half].wait()
        far_out[half] = jnp.dot(
            far_v[half], weight_v[...], preferred_element_type=jnp.float32
        ).astype(far_out.dtype)
        stores.append(
            pltpu.make_async_copy(far_out.at[half], out_ref.at[target + half], sems.at[3 + half])
        )
        stores[-1].start()
    for store in stores:
        store.wait()


def far_partial(place, weight, far, partial):
    width, units = weight.shape
    half = far[0].shape[0]
    return pl.pallas_call(
        far_kernel,
        in_specs=scalar() + lying(4),
        out_specs=lying(1)[0],
        out_shape=jax.ShapeDtypeStruct(partial.shape, partial.dtype),
        scratch_shapes=[
            pltpu.VMEM((width, units), jnp.bfloat16),
            pltpu.VMEM((2, half, width), jnp.bfloat16),
            pltpu.VMEM((2, half, units), jnp.bfloat16),
            pltpu.SemaphoreType.DMA((5,)),
        ],
        input_output_aliases={4: 0},
        compiler_params=params(),
    )(place, weight, *far, partial)


def last_kernel(weight_ref, rows_ref, out_ref):
    out_ref[...] = (
        jnp.dot(rows_ref[...], weight_ref[...], preferred_element_type=jnp.float32)
        .astype(out_ref.dtype)
        .reshape(out_ref.shape)
    )


def last_partial(weight, rows):
    return pl.pallas_call(
        last_kernel,
        in_specs=full(2),
        out_specs=full(1)[0],
        out_shape=jax.ShapeDtypeStruct(
            (PARTS, rows.shape[0] // PARTS, weight.shape[1]), jnp.bfloat16
        ),
        compiler_params=params(VMEM_LITTLE),
    )(weight, rows)


def weight_kernel(place_ref, hidden_ref, *refs):
    near, pieces = refs[:8], refs[8:-4]
    out_ref, rows_v, hidden_v, sems = refs[-4:]
    parts, _, size = hidden_ref.shape
    half = near[0].shape[0]
    slots = (size - half) // len(pieces)
    copies = []

    def fetch(piece, target, start, count, number):
        row = pl.multiple_of(target * size + start, slots)
        copies.append(
            pltpu.make_async_copy(
                piece, rows_v.at[pl.ds(row, count)], sems.at[number // parts, number % parts]
            )
        )

    for part in range(parts):
        copies.append(
            pltpu.make_async_copy(
                hidden_ref.at[part], hidden_v.at[:, pl.ds(part * size, size)], sems.at[0, part]
            )
        )
        for index, piece in enumerate(pieces):
            fetch(
                piece.at[pl.ds(part * slots, slots)],
                part,
                half + index * slots,
                slots,
                parts * (1 + index) + part,
            )
    for index, piece in enumerate(near):
        target = place_of(place_ref[0], (0, 3, 1, 2)[index // 2]) + index % 2
        fetch(piece, target, 0, half, parts * (1 + len(pieces)) + index)
    for copy in copies:
        copy.start()
    for copy in copies:
        copy.wait()
    out_ref[...] = jnp.dot(
        hidden_v[...], rows_v[...], preferred_element_type=jnp.float32
    ).astype(out_ref.dtype)


def weight_grad(place, hidden, near, far, pieces):
    parts, units, size = hidden.shape
    width = pieces[0].shape[1]
    return pl.pallas_call(
        weight_kernel,
        in_specs=scalar() + lying(9 + len(pieces)),
        out_specs=full(1)[0],
        out_shape=jax.ShapeDtypeStruct((units, width), jnp.bfloat16),
        scratch_shapes=[
            pltpu.VMEM((parts * size, width), jnp.bfloat16),
            pltpu.VMEM((units, parts * size), jnp.bfloat16),
            pltpu.SemaphoreType.DMA((2 + len(pieces), parts)),
        ],
        compiler_params=params(),
    )(place, hidden, *near, *far, *pieces)


def finish_kernel(sums_ref, last_ref, out_ref, sums_v, sem):
    copy = pltpu.make_async_copy(sums_ref, sums_v, sem)
    copy.start()
    last = jnp.sum(last_ref[...].astype(jnp.float32), axis=0).astype(jnp.bfloat16)
    copy.wait()
    joined = jnp.concatenate([sums_v[...], last], axis=0)
    size = joined.shape[0]
    first = lax.broadcasted_iota(jnp.int32, (size, size), 0)
    second = lax.broadcasted_iota(jnp.int32, (size, size), 1)
    same = jnp.where(first == second, 1.0, 0.0).astype(jnp.bfloat16)
    out_ref[...] = lax.dot_general(
        joined, same, (((0,), (0,)), ((), ())), preferred_element_type=jnp.float32
    ).astype(out_ref.dtype)


def finish(sums, last):
    slots, units = sums.shape
    return pl.pallas_call(
        finish_kernel,
        in_specs=lying(1) + full(1),
        out_specs=full(1)[0],
        out_shape=jax.ShapeDtypeStruct((units, slots + last.shape[1]), jnp.bfloat16),
        scratch_shapes=[pltpu.VMEM(sums.shape, sums.dtype), pltpu.SemaphoreType.DMA],
        compiler_params=params(VMEM_LITTLE),
    )(sums, last)


def shifted(value, axis, step):
    size = lax.axis_size(axis)
    return lax.ppermute(value, axis, [(i, (i + step) % size) for i in range(size)])


def per_device(out_grad, route_prob, expert_ids, slots, counts, down_weight, saved_hidden):
    flight = lax.axis_size("expert")
    edata = lax.axis_size("edata")
    width = out_grad.shape[1] // edata
    place = lax.axis_index("dp").astype(jnp.int32)[None]
    outgoing = dispatch(route_prob, expert_ids, slots, counts, out_grad, edata)
    arrived = lax.all_to_all(
        outgoing,
        ("edata", "expert"),
        split_axis=0,
        concat_axis=0,
        tiled=True,
    )
    arrived, hidden, weight = lax.optimization_barrier(
        (arrived, saved_hidden[0].T, turn(down_weight[0]))
    )
    hidden = lax.all_gather(hidden, "edata", axis=0)
    blocks = arrived.reshape(2, QUARTERS, -1, width)
    first = blocks[0, :3].reshape(-1, width)
    second = blocks[1, :3].reshape(-1, width)
    fourth = blocks[:, 3].reshape(-1, width)
    low_first = shifted(first, "dp", 1)
    high_second = shifted(second, "dp", -1)
    low_second = shifted(second, "dp", 1)
    high_first = shifted(first, "dp", -1)
    far = (shifted(low_first, "dp", 1), shifted(high_second, "dp", -1))
    near = (first, second, low_first, low_second, high_first, high_second)
    partial = near_partial(place, weight, near)
    partial = far_partial(place, weight, far, partial)
    partial, fourth, hidden = lax.optimization_barrier((partial, fourth, hidden))
    sums = lax.psum_scatter(partial, "edata", scatter_dimension=0, tiled=False)
    fourth = lax.all_gather(fourth, "dp", axis=0, tiled=True)
    spread = lax.all_to_all(
        last_partial(weight, fourth), "edata", split_axis=0, concat_axis=0, tiled=True
    )
    grad = weight_grad(place, hidden, near, far, (fourth,))
    return finish(sums, spread).T[None], grad[None]


def solution(mesh):
    placed = (
        P(("dp", "edata", "expert"), None),
        P(("dp", "edata", "expert"), None),
        P(("dp", "edata", "expert"), None),
        P(("dp", "edata", "expert"), None),
        P(("dp", "edata", "expert"), None),
        P("expert", "dp", "edata"),
        P("expert", "edata", "dp"),
    )
    return jax.shard_map(
        per_device,
        mesh=mesh,
        in_specs=placed,
        out_specs=(P("expert", "edata", "dp"), P("expert", "dp", "edata")),
        check_vma=False,
    )
```

```python
import jax
import jax.numpy as jnp
from jax import lax
from jax.experimental import pallas as pl
from jax.experimental.pallas import tpu as pltpu
from jax.sharding import PartitionSpec as P

EXP_DEV = 8
CAP = 4
PARTS = 8
QUARTERS = 4
VMEM_LIMIT = 60 * 1024 * 1024
VMEM_LITTLE = 20 * 1024 * 1024


def full(count):
    return [pl.BlockSpec(memory_space=pltpu.VMEM)] * count


def lying(count):
    return [pl.BlockSpec(memory_space=pl.ANY)] * count


def scalar():
    return [pl.BlockSpec(memory_space=pltpu.SMEM)]


def params(limit=VMEM_LIMIT):
    return pltpu.CompilerParams(vmem_limit_bytes=limit)


def dispatch_kernel(prob_ref, ids_ref, slots_ref, counts_ref, grad_ref, out_ref, *scratch):
    prob_v, ids_v, slots_v, counts_v, grad_v, out_v, sems, out_sems = scratch
    width = out_ref.shape[2]
    flight = counts_v.shape[1]
    rows = flight * CAP
    blocks = out_ref.shape[0] // flight
    tokens = grad_v.shape[1]
    copies = [
        pltpu.make_async_copy(source, place, sems.at[index])
        for index, (source, place) in enumerate(
            ((ids_ref, ids_v), (slots_ref, slots_v), (counts_ref, counts_v), (prob_ref, prob_v))
        )
    ]
    for block in range(blocks):
        copies.append(
            pltpu.make_async_copy(
                grad_ref.at[:, pl.ds(block * width, width)], grad_v.at[block], sems.at[4 + block]
            )
        )
    for copy in copies:
        copy.start()
    own = lax.broadcasted_iota(jnp.int32, (rows, flight), 0) // CAP
    column = lax.broadcasted_iota(jnp.int32, (rows, flight), 1)
    row = lax.broadcasted_iota(jnp.int32, (rows, tokens), 0)
    expert = (row // CAP) * EXP_DEV
    slot = row % CAP
    for copy in copies[:4]:
        copy.wait()
    limit = jnp.sum(jnp.where(own == column, counts_v[...], 0), axis=1, keepdims=True)
    picker = jnp.zeros((rows, tokens), jnp.float32)
    scale = jnp.zeros((rows, 1), jnp.float32)
    for choice in range(2):
        match = (
            (ids_v[choice : choice + 1, :] == expert)
            & (slots_v[choice : choice + 1, :] == slot)
            & (slot < limit)
        )
        picker = picker + jnp.where(match, 1.0, 0.0)
        scale = scale + jnp.sum(
            jnp.where(match, prob_v[choice : choice + 1, :], 0.0), axis=1, keepdims=True
        )
    picker = picker.astype(jnp.bfloat16)
    stores = []
    for block in range(blocks):
        copies[4 + block].wait()
        picked = jnp.dot(picker, grad_v[block], preferred_element_type=jnp.float32)
        window = pl.ds(block * flight, flight)
        out_v[window] = (picked * scale).reshape(flight, CAP, width).astype(out_v.dtype)
        stores.append(
            pltpu.make_async_copy(out_v.at[window], out_ref.at[window], out_sems.at[block])
        )
        stores[-1].start()
    for store in stores:
        store.wait()


def dispatch(route_prob, expert_ids, slots, counts, out_grad, blocks):
    tokens, model = out_grad.shape
    flight = counts.shape[1]
    width = model // blocks
    return pl.pallas_call(
        dispatch_kernel,
        in_specs=lying(5),
        out_specs=lying(1)[0],
        out_shape=jax.ShapeDtypeStruct((blocks * flight, CAP, width), jnp.bfloat16),
        scratch_shapes=[
            pltpu.VMEM((2, tokens), jnp.float32),
            pltpu.VMEM((2, tokens), jnp.int32),
            pltpu.VMEM((2, tokens), jnp.int32),
            pltpu.VMEM((1, flight), jnp.int32),
            pltpu.VMEM((blocks, tokens, width), jnp.bfloat16),
            pltpu.VMEM((blocks * flight, CAP, width), jnp.bfloat16),
            pltpu.SemaphoreType.DMA((4 + blocks,)),
            pltpu.SemaphoreType.DMA((blocks,)),
        ],
        compiler_params=params(),
    )(route_prob.T, expert_ids.T, slots.T, counts, out_grad)


def turn_kernel(weight_ref, out_ref):
    out_ref[...] = weight_ref[...].T


def turn(weight):
    units, width = weight.shape
    return pl.pallas_call(
        turn_kernel,
        in_specs=full(1),
        out_specs=full(1)[0],
        out_shape=jax.ShapeDtypeStruct((width, units), weight.dtype),
        compiler_params=params(),
    )(weight)


def place_of(place, shift):
    return lax.rem(place + shift, PARTS // 2) * 2


def near_kernel(place_ref, weight_ref, *refs):
    pieces = refs[:6]
    out_ref, weight_v, near_v, near_out, sems, out_sems = refs[6:]
    _, half, units = out_ref.shape
    load = pltpu.make_async_copy(weight_ref, weight_v, sems.at[6])
    load.start()
    copies = [
        pltpu.make_async_copy(
            piece, near_v.at[index // 2, pl.ds(index % 2 * half, half)], sems.at[index]
        )
        for index, piece in enumerate(pieces)
    ]
    for copy in copies:
        copy.start()
    load.wait()
    stores = []
    for index, shift in enumerate((0, 3, 1)):
        copies[2 * index].wait()
        copies[2 * index + 1].wait()
        near_out[index] = (
            jnp.dot(near_v[index], weight_v[...], preferred_element_type=jnp.float32)
            .astype(near_out.dtype)
            .reshape(2, half, units)
        )
        stores.append(
            pltpu.make_async_copy(
                near_out.at[index],
                out_ref.at[pl.ds(place_of(place_ref[0], shift), 2)],
                out_sems.at[index],
            )
        )
        stores[-1].start()
    for store in stores:
        store.wait()


def near_partial(place, weight, near):
    width, units = weight.shape
    half = near[0].shape[0]
    return pl.pallas_call(
        near_kernel,
        in_specs=scalar() + lying(7),
        out_specs=lying(1)[0],
        out_shape=jax.ShapeDtypeStruct((PARTS, half, units), jnp.bfloat16),
        scratch_shapes=[
            pltpu.VMEM((width, units), jnp.bfloat16),
            pltpu.VMEM((3, 2 * half, width), jnp.bfloat16),
            pltpu.VMEM((3, 2, half, units), jnp.bfloat16),
            pltpu.SemaphoreType.DMA((7,)),
            pltpu.SemaphoreType.DMA((3,)),
        ],
        compiler_params=params(),
    )(place, weight, *near)


def far_kernel(place_ref, weight_ref, first_ref, second_ref, _, out_ref, *scratch):
    weight_v, far_v, far_out, sems = scratch
    target = place_of(place_ref[0], 2)
    width = weight_v.shape[0]
    cut = width // 2 // 128 * 128
    spans = ((0, cut), (cut, width - cut))
    loads = [
        pltpu.make_async_copy(
            weight_ref.at[pl.ds(*span)], weight_v.at[pl.ds(*span)], sems.at[5 * index]
        )
        for index, span in enumerate(spans)
    ]
    loads[0].start()
    copies = [
        pltpu.make_async_copy(piece, far_v.at[half], sems.at[1 + half])
        for half, piece in enumerate((first_ref, second_ref))
    ]
    for copy in copies:
        copy.start()
    loads[1].start()
    loads[0].wait()
    stores = []
    for half in range(2):
        copies[half].wait()
        product = jnp.dot(
            far_v[half, :, :cut], weight_v[:cut], preferred_element_type=jnp.float32
        )
        if half == 0:
            loads[1].wait()
        product += jnp.dot(
            far_v[half, :, cut:], weight_v[cut:], preferred_element_type=jnp.float32
        )
        far_out[half] = product.astype(far_out.dtype)
        stores.append(
            pltpu.make_async_copy(far_out.at[half], out_ref.at[target + half], sems.at[3 + half])
        )
        stores[-1].start()
    for store in stores:
        store.wait()


def far_partial(place, weight, far, partial):
    width, units = weight.shape
    half = far[0].shape[0]
    return pl.pallas_call(
        far_kernel,
        in_specs=scalar() + lying(4),
        out_specs=lying(1)[0],
        out_shape=jax.ShapeDtypeStruct(partial.shape, partial.dtype),
        scratch_shapes=[
            pltpu.VMEM((width, units), jnp.bfloat16),
            pltpu.VMEM((2, half, width), jnp.bfloat16),
            pltpu.VMEM((2, half, units), jnp.bfloat16),
            pltpu.SemaphoreType.DMA((6,)),
        ],
        input_output_aliases={4: 0},
        compiler_params=params(),
    )(place, weight, *far, partial)


def last_kernel(weight_ref, rows_ref, out_ref):
    out_ref[...] = (
        jnp.dot(rows_ref[...], weight_ref[...], preferred_element_type=jnp.float32)
        .astype(out_ref.dtype)
        .reshape(out_ref.shape)
    )


def last_partial(weight, rows):
    return pl.pallas_call(
        last_kernel,
        in_specs=full(2),
        out_specs=full(1)[0],
        out_shape=jax.ShapeDtypeStruct(
            (PARTS, rows.shape[0] // PARTS, weight.shape[1]), jnp.bfloat16
        ),
        compiler_params=params(VMEM_LITTLE),
    )(weight, rows)


def weight_kernel(place_ref, hidden_ref, *refs):
    near, pieces = refs[:8], refs[8:-4]
    out_ref, rows_v, hidden_v, sems = refs[-4:]
    parts, _, size = hidden_ref.shape
    half = near[0].shape[0]
    slots = (size - half) // len(pieces)
    copies = []

    def fetch(piece, target, start, count, number):
        row = pl.multiple_of(target * size + start, slots)
        copies.append(
            pltpu.make_async_copy(
                piece, rows_v.at[pl.ds(row, count)], sems.at[number // parts, number % parts]
            )
        )

    for part in range(parts):
        copies.append(
            pltpu.make_async_copy(
                hidden_ref.at[part], hidden_v.at[:, pl.ds(part * size, size)], sems.at[0, part]
            )
        )
        for index, piece in enumerate(pieces):
            fetch(
                piece.at[pl.ds(part * slots, slots)],
                part,
                half + index * slots,
                slots,
                parts * (1 + index) + part,
            )
    for index, piece in enumerate(near):
        target = place_of(place_ref[0], (0, 3, 1, 2)[index // 2]) + index % 2
        fetch(piece, target, 0, half, parts * (1 + len(pieces)) + index)
    for copy in copies:
        copy.start()
    for copy in copies:
        copy.wait()
    out_ref[...] = jnp.dot(
        hidden_v[...], rows_v[...], preferred_element_type=jnp.float32
    ).astype(out_ref.dtype)


def weight_grad(place, hidden, near, far, pieces):
    parts, units, size = hidden.shape
    width = pieces[0].shape[1]
    return pl.pallas_call(
        weight_kernel,
        in_specs=scalar() + lying(9 + len(pieces)),
        out_specs=full(1)[0],
        out_shape=jax.ShapeDtypeStruct((units, width), jnp.bfloat16),
        scratch_shapes=[
            pltpu.VMEM((parts * size, width), jnp.bfloat16),
            pltpu.VMEM((units, parts * size), jnp.bfloat16),
            pltpu.SemaphoreType.DMA((2 + len(pieces), parts)),
        ],
        compiler_params=params(),
    )(place, hidden, *near, *far, *pieces)


def finish_kernel(sums_ref, last_ref, out_ref, sums_v, sem):
    copy = pltpu.make_async_copy(sums_ref, sums_v, sem)
    copy.start()
    last = jnp.sum(last_ref[...].astype(jnp.float32), axis=0).astype(jnp.bfloat16)
    copy.wait()
    joined = jnp.concatenate([sums_v[...], last], axis=0)
    size = joined.shape[0]
    first = lax.broadcasted_iota(jnp.int32, (size, size), 0)
    second = lax.broadcasted_iota(jnp.int32, (size, size), 1)
    same = jnp.where(first == second, 1.0, 0.0).astype(jnp.bfloat16)
    out_ref[...] = lax.dot_general(
        joined, same, (((0,), (0,)), ((), ())), preferred_element_type=jnp.float32
    ).astype(out_ref.dtype)


def finish(sums, last):
    slots, units = sums.shape
    return pl.pallas_call(
        finish_kernel,
        in_specs=lying(1) + full(1),
        out_specs=full(1)[0],
        out_shape=jax.ShapeDtypeStruct((units, slots + last.shape[1]), jnp.bfloat16),
        scratch_shapes=[pltpu.VMEM(sums.shape, sums.dtype), pltpu.SemaphoreType.DMA],
        compiler_params=params(VMEM_LITTLE),
    )(sums, last)


def shifted(value, axis, step):
    size = lax.axis_size(axis)
    return lax.ppermute(value, axis, [(i, (i + step) % size) for i in range(size)])


def per_device(out_grad, route_prob, expert_ids, slots, counts, down_weight, saved_hidden):
    flight = lax.axis_size("expert")
    edata = lax.axis_size("edata")
    width = out_grad.shape[1] // edata
    place = lax.axis_index("dp").astype(jnp.int32)[None]
    outgoing = dispatch(route_prob, expert_ids, slots, counts, out_grad, edata)
    arrived = lax.all_to_all(
        outgoing,
        ("edata", "expert"),
        split_axis=0,
        concat_axis=0,
        tiled=True,
    )
    arrived, hidden, weight = lax.optimization_barrier(
        (arrived, saved_hidden[0].T, turn(down_weight[0]))
    )
    hidden = lax.all_gather(hidden, "edata", axis=0)
    blocks = arrived.reshape(2, QUARTERS, -1, width)
    first = blocks[0, :3].reshape(-1, width)
    second = blocks[1, :3].reshape(-1, width)
    fourth = blocks[:, 3].reshape(-1, width)
    low_first = shifted(first, "dp", 1)
    high_second = shifted(second, "dp", -1)
    low_second = shifted(second, "dp", 1)
    high_first = shifted(first, "dp", -1)
    far = (shifted(low_first, "dp", 1), shifted(high_second, "dp", -1))
    near = (first, second, low_first, low_second, high_first, high_second)
    partial = near_partial(place, weight, near)
    partial = far_partial(place, weight, far, partial)
    partial, fourth, hidden = lax.optimization_barrier((partial, fourth, hidden))
    sums = lax.psum_scatter(partial, "edata", scatter_dimension=0, tiled=False)
    fourth = lax.all_gather(fourth, "dp", axis=0, tiled=True)
    spread = lax.all_to_all(
        last_partial(weight, fourth), "edata", split_axis=0, concat_axis=0, tiled=True
    )
    grad = weight_grad(place, hidden, near, far, (fourth,))
    return finish(sums, spread).T[None], grad[None]


def solution(mesh):
    placed = (
        P(("dp", "edata", "expert"), None),
        P(("dp", "edata", "expert"), None),
        P(("dp", "edata", "expert"), None),
        P(("dp", "edata", "expert"), None),
        P(("dp", "edata", "expert"), None),
        P("expert", "dp", "edata"),
        P("expert", "edata", "dp"),
    )
    return jax.shard_map(
        per_device,
        mesh=mesh,
        in_specs=placed,
        out_specs=(P("expert", "edata", "dp"), P("expert", "dp", "edata")),
        check_vma=False,
    )
```
